32 devices in a mesh: groups: 2 (over y), expert: 8 (over z, x), tensor: 2 (over core).
Axes of the slice: x: 2, y: 2, z: 4, core: 2. Of those that a mesh axis runs over, the one named last changes fastest.
Arguments:
- conv_input: bfloat16 [32, 8192], P(('groups', 'expert'), 'tensor'), parts along dimension 0, may hold values from -6 to 6
- gate_input: bfloat16 [32, 8192], P(('groups', 'expert'), 'tensor'), parts along dimension 0, may hold values from -6 to 6
- step_input: bfloat16 [32, 8192], P(('groups', 'expert'), 'tensor'), parts along dimension 0, may hold values from -6 to 6
- b_proj: float32 [32, 16], P(('groups', 'expert')), parts along dimension 0, may hold values from -6 to 6
- c_proj: float32 [32, 16], P(('groups', 'expert')), parts along dimension 0, may hold values from -6 to 6
- slot_ids: int32 [32], P(('groups', 'expert')), parts along dimension 0, may hold values from 0 to 15, as said below
- state_pool: bfloat16 [32, 16, 8192], P(('groups', 'expert'), None, 'tensor'), parts along dimension 0, may hold values from -6 to 6
- conv_pool: bfloat16 [32, 3, 8192], P(('groups', 'expert'), None, 'tensor'), parts along dimension 0, may hold values from -6 to 6
- conv_weight: float32 [4, 8192], P(None, 'tensor'), may hold values from -4 to 4
- conv_bias: float32 [8192], P('tensor'), may hold values from -4 to 4
- step_bias: float32 [8192], P('tensor'), may hold values from -4 to 0
- a_log: float32 [16, 8192], P(None, 'tensor'), may hold values from -1 to 2.5
- d_skip: float32 [8192], P('tensor'), may hold values from 0.5 to 1.5
- out_weight: bfloat16 [8192, 4096], P('tensor', 'expert'), may hold values from -0.0625 to 0.0625
- residual: bfloat16 [32, 4096], P(('groups', 'expert')), parts along dimension 0, may hold values from -6 to 6
- norm_gain: float32 [4096], replicated, may hold values from 0.5 to 1.5
- expert_ids: int32 [32, 2], P(('groups', 'expert')), parts along dimension 0, may hold values from 0 to 2, all different within a row
- expert_probs: bfloat16 [32, 2], P(('groups', 'expert')), parts along dimension 0, may hold values from 0.19921875 to 1
- gate_weight: bfloat16 [36864, 4096], P(('expert', 'tensor')), may hold values from -0.09375 to 0.09375
- up_weight: bfloat16 [36864, 4096], P(('expert', 'tensor')), may hold values from -0.09375 to 0.09375
- down_weight: bfloat16 [36864, 4096], P(('expert', 'tensor')), may hold values from -0.0546875 to 0.0546875
Outputs:
- layer_out: bfloat16 [32, 4096], P(('groups', 'expert')), parts along dimension 0
- new_state: bfloat16 [32, 16, 8192], P(('groups', 'expert'), None, 'tensor'), parts along dimension 0
The draws below stay inside these ranges and needn't reach their ends.
There are 2 independent parts, one for each index of `groups`. The reference program is written for one: setup_inputs(seed, part) draws one part's arguments, and reference() takes and returns one part's arrays. A program takes and returns all parts, laid end to end along the dimension named above; an argument that names none is the same for every part. Nothing has to cross between parts.
Inputs may be any that keep to these rules, and one draw needn't show every extreme that they name: `slot_ids`: the rows of one index of expert (rows d*2 to (d+1)*2 - 1) use distinct slots among d*2 to (d+1)*2 - 1. `expert_ids`: each row names two different experts.
All inputs are finite; a program needn't handle non-finite values.
Results may differ from the reference program's by a relative error of at most 0.0063.
Values may be sent and summed in bfloat16 or wider, within the bound.
No kernel may reach another device: no remote copies, remote signals or barrier semaphores. Data moves between devices by JAX's collectives and lax.ppermute only.
A program may use at most 128 MiB of HBM per device.

```python
import jax
import jax.numpy as jnp
from jax import lax

D = 4096
CH = 8192
NS = 16
KC = 4
EXPERTS = 3
FF = 12288
ROWS_DEV = 2
POOL_DEV = 2
ROWS = 16
SLOTS = 16


def draw_slot_ids(key, part):
    devices = ROWS // ROWS_DEV
    scores = jax.random.randint(key, (devices, POOL_DEV), 0, 1 << 20)
    scores = scores * POOL_DEV + jnp.arange(POOL_DEV, dtype=jnp.int32)[None, :]
    ranking = jnp.argsort(scores, axis=1).astype(jnp.int32)
    chosen = ranking[:, :ROWS_DEV] + (jnp.arange(devices, dtype=jnp.int32) * POOL_DEV)[:, None]
    return chosen.reshape(ROWS).astype(jnp.int32)


def steps_of(key, shape, pieces, low, largest):
    def one(position, parts):
        draws = jax.random.uniform(jax.random.fold_in(jax.random.fold_in(key, 6), position), (parts,), jnp.float32, low / len(pieces), largest / len(pieces))
        return jnp.repeat(jnp.exp(draws), shape[position] // parts).reshape((-1,) + (1,) * (len(shape) - position - 1))

    gain = one(*pieces[0])
    for cut in pieces[1:]:
        gain = gain * one(*cut)
    return gain


def distinct(own_key, rows, number_of, top, lift):
    order = jax.random.permutation(jax.random.fold_in(own_key, 1), number_of)
    favour = order
    for power in range(3):
        favour = favour * favour // number_of
    favour = favour * lift // number_of
    tickets = jax.random.randint(jax.random.fold_in(own_key, 2), (rows, number_of), 0, 4096) + favour
    sure = jax.random.permutation(jax.random.fold_in(own_key, 3), rows)[jnp.arange(number_of) % rows]
    tickets = jnp.where(jnp.arange(rows)[:, None] == sure[None, :], 1 << 14, tickets)
    merit = tickets * number_of + jnp.arange(number_of)
    return lax.top_k(merit.astype(jnp.int32), top)[1].astype(jnp.int32)


def normal_values(own_key, shape, deviation, bound, shards=(), kind=jnp.bfloat16):
    factor_of = steps_of(own_key, shape, shards, -0.22, 0.18) if shards else 1.0
    values = jax.random.normal(own_key, shape, jnp.float32) * deviation * factor_of
    return jnp.minimum(jnp.maximum(values, -bound), bound).astype(kind)


def setup_inputs(seed: int = 0, part: int = 0) -> dict:
    streams_of = jax.random.split(jax.random.key(seed), 22)
    part_keys = jax.random.split(jax.random.fold_in(streams_of[21], part), 22)
    return {
        "conv_input": normal_values(part_keys[0], (ROWS, CH), 1.0, 6.0, ((0, 8), (1, 2))),
        "gate_input": normal_values(part_keys[1], (ROWS, CH), 1.0, 6.0, ((0, 8), (1, 2))),
        "step_input": normal_values(part_keys[2], (ROWS, CH), 1.0, 6.0, ((0, 8), (1, 2))),
        "b_proj": normal_values(part_keys[3], (ROWS, NS), 1.0, 6.0, ((0, 8),), jnp.float32),
        "c_proj": normal_values(part_keys[4], (ROWS, NS), 0.5, 6.0, ((0, 8),), jnp.float32),
        "slot_ids": draw_slot_ids(jax.random.fold_in(jax.random.fold_in(streams_of[21], part), 71), part),
        "state_pool": normal_values(part_keys[6], (SLOTS, NS, CH), 1.0, 6.0, ((0, 8), (2, 2))),
        "conv_pool": normal_values(part_keys[7], (SLOTS, KC - 1, CH), 1.0, 6.0, ((0, 8), (2, 2))),
        "conv_weight": normal_values(streams_of[8], (KC, CH), 0.5, 4.0, ((1, 2),), jnp.float32),
        "conv_bias": normal_values(streams_of[9], (CH,), 0.5, 4.0, ((0, 2),), jnp.float32),
        "step_bias": jnp.clip(-4.0 + 4.0 * jax.random.uniform(streams_of[10], (CH,), jnp.float32) ** steps_of(streams_of[10], (CH,), ((0, 2),), -0.2, 0.2), -4.0, 0.0),
        "a_log": jnp.clip(-1.0 + 3.5 * jax.random.uniform(streams_of[11], (NS, CH), jnp.float32) ** steps_of(streams_of[11], (NS, CH), ((1, 2),), -0.2, 0.2), -1.0, 2.5),
        "d_skip": jnp.clip(0.5 + 1.0 * jax.random.uniform(streams_of[12], (CH,), jnp.float32) ** steps_of(streams_of[12], (CH,), ((0, 2),), -0.2, 0.2), 0.5, 1.5),
        "out_weight": normal_values(streams_of[13], (CH, D), CH ** -0.5, 0.0625, ((0, 2), (1, 8))),
        "residual": normal_values(part_keys[14], (ROWS, D), 1.0, 6.0, ((0, 8),)),
        "norm_gain": jnp.clip(1.0 + 0.1 * jax.random.normal(streams_of[15], (D,), jnp.float32), 0.5, 1.5),
        "expert_ids": distinct(part_keys[16], ROWS, EXPERTS, 2, 10922),
        "expert_probs": jnp.clip(0.19921875 + 0.80078125 * jax.random.uniform(part_keys[17], (ROWS, 2), jnp.float32) ** steps_of(part_keys[17], (ROWS, 2), ((0, 8),), -0.2, 0.2), 0.19921875, 1.0).astype(jnp.bfloat16),
        "gate_weight": normal_values(streams_of[18], (EXPERTS * FF, D), D ** -0.5, 0.09375, ((0, 16),)),
        "up_weight": normal_values(streams_of[19], (EXPERTS * FF, D), D ** -0.5, 0.09375, ((0, 16),)),
        "down_weight": normal_values(streams_of[20], (EXPERTS * FF, D), FF ** -0.5, 0.0546875, ((0, 16),)),
    }


def mamba_step(states, history, conv_input, gate_input, step_input, b_proj, c_proj, conv_weight, conv_bias, step_bias, a_log, d_skip):
    inputs = conv_input.astype(jnp.float32)
    conv_sum = conv_weight[-1] * inputs + conv_bias
    for lag in range(history.shape[1]):
        conv_sum = conv_sum + conv_weight[lag] * history[:, lag]
    conv_out = jax.nn.silu(conv_sum)
    step_size = jax.nn.softplus(step_input.astype(jnp.float32) + step_bias)
    state_rates = -jnp.exp(a_log)
    decay_rate = jnp.exp(step_size[:, None, :] * state_rates[None])
    state_next = decay_rate * states + (step_size * conv_out)[:, None, :] * b_proj[:, :, None]
    output = lax.optimization_barrier(jnp.sum(c_proj[:, :, None] * state_next, axis=1)) + d_skip * conv_out
    gated_out = (output * jax.nn.silu(gate_input.astype(jnp.float32))).astype(jnp.bfloat16)
    return (state_next, gated_out)

def expert_ffn(rows, gate_part, up_part, down_part):
    dims = (((1,), (1,)), ((), ()))
    gate_act = lax.dot_general(rows, gate_part, dims, preferred_element_type=jnp.float32)
    up_act = lax.dot_general(rows, up_part, dims, preferred_element_type=jnp.float32)
    hidden = (jax.nn.silu(gate_act) * up_act).astype(jnp.bfloat16)
    return jnp.dot(hidden, down_part, preferred_element_type=jnp.float32)

def reference(conv_input, gate_input, step_input, b_proj, c_proj, slot_ids, state_pool, conv_pool, conv_weight, conv_bias, step_bias, a_log, d_skip, out_weight, residual, norm_gain, expert_ids, expert_probs, gate_weight, up_weight, down_weight):
    states = state_pool[slot_ids].astype(jnp.float32)
    history = conv_pool[slot_ids].astype(jnp.float32)
    state_next, gated_out = mamba_step(states, history, conv_input, gate_input, step_input, b_proj, c_proj, conv_weight, conv_bias, step_bias, a_log, d_skip)
    mixed = jnp.dot(gated_out, out_weight, preferred_element_type=jnp.float32).astype(jnp.bfloat16)
    hidden_state = (residual.astype(jnp.float32) + mixed.astype(jnp.float32)).astype(jnp.bfloat16)
    wide = hidden_state.astype(jnp.float32)
    normed = (wide * lax.rsqrt(lax.optimization_barrier(jnp.mean(wide * wide, axis=1, keepdims=True)) + 1e-05) * norm_gain).astype(jnp.bfloat16)
    probs = expert_probs.astype(jnp.float32)

    def one_expert(carry, expert):
        start = (expert * FF).astype(jnp.int32)
        gate_part = lax.dynamic_slice_in_dim(gate_weight, start, FF, 0)
        up_part = lax.dynamic_slice_in_dim(up_weight, start, FF, 0)
        down_part = lax.dynamic_slice_in_dim(down_weight, start, FF, 0)
        result = expert_ffn(normed, gate_part, up_part, down_part)
        weight_row = lax.optimization_barrier(jnp.sum(probs * (expert_ids == expert).astype(jnp.float32), axis=1))
        return (carry + weight_row[:, None] * result, None)
    routed, _ = lax.scan(one_expert, jnp.zeros((normed.shape[0], normed.shape[1]), jnp.float32), jnp.arange(EXPERTS, dtype=jnp.int32))
    layer_out = (hidden_state.astype(jnp.float32) + routed).astype(jnp.bfloat16)
    return (layer_out, state_next.astype(jnp.bfloat16))
```

```python
import jax
import jax.numpy as jnp
from jax import lax
from jax.experimental import pallas as pl
from jax.experimental.pallas import tpu as pltpu
from jax.sharding import PartitionSpec as P

EXPERTS = 3
FF = 12288


def mamba_step(
    states,
    history,
    conv_input,
    gate_input,
    step_input,
    b_proj,
    c_proj,
    conv_weight,
    conv_bias,
    step_bias,
    a_log,
    d_skip,
):
    inputs = conv_input.astype(jnp.float32)
    conv_sum = conv_weight[-1] * inputs + conv_bias
    for lag in range(history.shape[1]):
        conv_sum = conv_sum + conv_weight[lag] * history[:, lag]
    conv_out = jax.nn.silu(conv_sum)
    step_size = jax.nn.softplus(step_input.astype(jnp.float32) + step_bias)
    state_rates = -jnp.exp(a_log)
    decay_rate = jnp.exp(step_size[:, None, :] * state_rates[None])
    state_next = decay_rate * states + (step_size * conv_out)[:, None, :] * b_proj[:, :, None]
    output = jnp.sum(c_proj[:, :, None] * state_next, axis=1) + d_skip * conv_out
    gated_out = (output * jax.nn.silu(gate_input.astype(jnp.float32))).astype(jnp.bfloat16)
    return (state_next, gated_out)


def expert_terms(rows, coefs, first_unit, gate_weight, up_weight, down_weight):
    dims = (((1,), (1,)), ((), ()))
    gate_act = lax.dot_general(rows, gate_weight, dims, preferred_element_type=jnp.float32)
    up_act = lax.dot_general(rows, up_weight, dims, preferred_element_type=jnp.float32)
    hidden = (jax.nn.silu(gate_act) * up_act).astype(jnp.bfloat16)
    units = gate_weight.shape[0]
    lower_expert = first_unit // FF
    boundary = (lower_expert + 1) * FF - first_unit
    column = jnp.arange(units, dtype=jnp.int32)[None, :]
    zeros_bf = jnp.zeros_like(hidden)
    lower_hidden = jnp.where(column < boundary, hidden, zeros_bf)
    upper_hidden = jnp.where(column >= boundary, hidden, zeros_bf)
    expert_range = jnp.arange(EXPERTS, dtype=jnp.int32)[None, :]
    wide_coefs = coefs.astype(jnp.float32)
    lower_coef = jnp.sum(wide_coefs * (expert_range == lower_expert).astype(jnp.float32), axis=1)
    upper_coef = jnp.sum(
        wide_coefs * (expert_range == lower_expert + 1).astype(jnp.float32), axis=1
    )
    lower_out = jnp.dot(lower_hidden, down_weight, preferred_element_type=jnp.float32)
    upper_out = jnp.dot(upper_hidden, down_weight, preferred_element_type=jnp.float32)
    return lower_coef[:, None] * lower_out + upper_coef[:, None] * upper_out


def local(
    conv_input,
    gate_input,
    step_input,
    b_proj,
    c_proj,
    slot_ids,
    state_pool,
    conv_pool,
    conv_weight,
    conv_bias,
    step_bias,
    a_log,
    d_skip,
    out_weight,
    residual,
    norm_gain,
    expert_ids,
    expert_probs,
    gate_weight,
    up_weight,
    down_weight,
):
    pool_dev = state_pool.shape[0]
    local_slot = slot_ids - lax.axis_index("expert") * pool_dev
    select = (local_slot[:, None] == jnp.arange(pool_dev, dtype=jnp.int32)[None, :]).astype(
        jnp.bfloat16
    )
    states = jnp.einsum("rp,pnc->rnc", select, state_pool, preferred_element_type=jnp.float32)
    history = jnp.einsum("rp,pkc->rkc", select, conv_pool, preferred_element_type=jnp.float32)
    state_next, gated_out = mamba_step(
        states,
        history,
        conv_input,
        gate_input,
        step_input,
        b_proj,
        c_proj,
        conv_weight,
        conv_bias,
        step_bias,
        a_log,
        d_skip,
    )
    columns = jnp.dot(
        lax.all_gather(gated_out, "expert", axis=0, tiled=True),
        out_weight,
        preferred_element_type=jnp.float32,
    )
    returned_cols = lax.all_to_all(columns, "expert", split_axis=0, concat_axis=1, tiled=True)
    mixed = lax.psum(returned_cols, "tensor").astype(jnp.bfloat16)
    hidden_state = (residual.astype(jnp.float32) + mixed.astype(jnp.float32)).astype(jnp.bfloat16)
    wide = hidden_state.astype(jnp.float32)
    normed = (
        wide * lax.rsqrt(jnp.mean(wide * wide, axis=1, keepdims=True) + 1e-05) * norm_gain
    ).astype(jnp.bfloat16)
    probs = expert_probs.astype(jnp.float32)
    expert_range = jnp.arange(EXPERTS, dtype=jnp.int32)
    picked = (expert_ids[:, :, None] == expert_range[None, None, :]).astype(jnp.float32)
    coefs = jnp.sum(picked * probs[:, :, None], axis=1).astype(jnp.bfloat16)
    units = gate_weight.shape[0]
    first_unit = (
        lax.axis_index("expert") * lax.axis_size("tensor") + lax.axis_index("tensor")
    ) * units
    peers = lax.axis_size("expert")
    span = EXPERTS * FF // peers
    dest = jnp.arange(peers, dtype=jnp.int32)[:, None]
    intersection = (
        (expert_range[None, :] * FF < (dest + 1) * span)
        & ((expert_range[None, :] + 1) * FF > dest * span)
    ).astype(jnp.float32)
    chosen = jnp.sum(picked, axis=1)
    needed = jnp.dot(intersection, chosen.T, preferred_element_type=jnp.float32) > 0.5
    outgoing = jnp.where(needed[:, :, None], normed[None], jnp.zeros_like(normed)[None])
    out_coefs = jnp.broadcast_to(coefs[None], (peers, coefs.shape[0], coefs.shape[1]))
    rows_in = lax.all_to_all(outgoing, "expert", split_axis=0, concat_axis=0, tiled=True)
    coefs_in = lax.all_to_all(out_coefs, "expert", split_axis=0, concat_axis=0, tiled=True)
    flat_rows = rows_in.reshape(-1, rows_in.shape[2])
    flat_coefs = coefs_in.reshape(-1, coefs_in.shape[2])
    result = expert_terms(flat_rows, flat_coefs, first_unit, gate_weight, up_weight, down_weight)
    partial_value = result.reshape(rows_in.shape[0], rows_in.shape[1], rows_in.shape[2])
    returned = lax.all_to_all(partial_value, "expert", split_axis=0, concat_axis=0, tiled=True)
    routed = lax.psum(jnp.sum(returned, axis=0), "tensor")
    layer_out = (hidden_state.astype(jnp.float32) + routed).astype(jnp.bfloat16)
    return (layer_out, state_next.astype(jnp.bfloat16))


LANES = 128
BLOCK = 256
EPS = 1e-05
VMEM = pl.BlockSpec(memory_space=pltpu.VMEM)
SMEM = pl.BlockSpec(memory_space=pltpu.SMEM)
ANY = pl.BlockSpec(memory_space=pl.ANY)
F32 = jnp.float32
BF16 = jnp.bfloat16


def lane_to_sublane(row):
    n = row.shape[1]
    spread = jnp.broadcast_to(row, (n, n))
    diagonal = lax.broadcasted_iota(jnp.int32, (n, n), 0) == lax.broadcasted_iota(
        jnp.int32, (n, n), 1
    )
    return jnp.sum(jnp.where(diagonal, spread, 0.0), axis=1, keepdims=True)


def mixer_kernel(
    slot_ref,
    ids_ref,
    conv_input,
    gate_input,
    step_input,
    b_proj,
    c_proj,
    state_pool,
    conv_pool,
    conv_weight,
    conv_bias,
    step_bias,
    a_log,
    d_skip,
    residual,
    probs,
    new_state,
    packet,
):
    rows, channels = conv_input.shape
    peers = packet.shape[0]
    cols = residual.shape[1] // peers
    first_slot = lax.axis_index("expert") * state_pool.shape[0]
    rates = -jnp.exp(a_log[...])
    lane = lax.broadcasted_iota(jnp.int32, (1, LANES), 1)
    for r in range(rows):
        slot = slot_ref[r] - first_slot
        conv = conv_weight[-1:, :] * conv_input[r : r + 1, :].astype(F32) + conv_bias[...]
        for lag in range(conv_pool.shape[0]):
            past = conv_pool[lag].astype(F32)
            picked = lax.broadcasted_iota(jnp.int32, past.shape, 0) == slot
            history = jnp.sum(jnp.where(picked, past, 0.0), axis=0, keepdims=True)
            conv = conv + conv_weight[lag : lag + 1, :] * history
        conv_out = conv * jax.nn.sigmoid(conv)
        step = jax.nn.softplus(step_input[r : r + 1, :].astype(F32) + step_bias[...])
        b = lane_to_sublane(b_proj[r : r + 1, :])
        c = lane_to_sublane(c_proj[r : r + 1, :])
        state = jnp.exp(step * rates) * state_pool[slot].astype(F32) + (step * conv_out) * b
        new_state[r] = state.astype(BF16)
        output = jnp.sum(c * state, axis=0, keepdims=True) + d_skip[...] * conv_out
        gate = gate_input[r : r + 1, :].astype(F32)
        gated = (output * (gate * jax.nn.sigmoid(gate))).astype(BF16)
        coefs = jnp.zeros((1, LANES), F32)
        for k in range(ids_ref.shape[1]):
            coefs = coefs + jnp.where(lane == ids_ref[r, k], probs[r, k], 0.0)
        coefs = coefs.astype(BF16)
        for d in range(peers):
            packet[d, r : r + 1, 0:channels] = gated
            packet[d, r : r + 1, channels : channels + cols] = residual[
                r : r + 1, d * cols : (d + 1) * cols
            ]
            packet[d, r : r + 1, channels + cols :] = coefs


def project_kernel(packets, out_weight, partial, residual_block, coefs, rows_scratch):
    peers, rows, _ = packets.shape
    channels, cols = out_weight.shape
    for d in range(peers):
        rows_scratch[d * rows : (d + 1) * rows, :] = packets[d].astype(F32)
    partial[...] = jnp.dot(
        rows_scratch[:, 0:channels].astype(BF16), out_weight[...], preferred_element_type=F32
    )
    residual_block[...] = rows_scratch[:, channels : channels + cols]
    coefs[...] = rows_scratch[:, channels + cols :]


def hidden_kernel(mine, other, residual_block, copies):
    mixed = (mine[...] + other[...]).astype(BF16).astype(F32)
    hidden = (residual_block[...] + mixed).astype(BF16)
    for d in range(copies.shape[0]):
        copies[d] = hidden


def expert_kernel(
    hidden,
    coefs,
    gain,
    gate_hbm,
    up_hbm,
    down_hbm,
    partial,
    own_rows,
    gate_buf,
    up_buf,
    down_buf,
    wide,
    normed,
    units_out,
    total,
    gate_sem,
    up_sem,
    down_sem,
):
    units, width = gate_buf.shape
    peers, rows, cols = hidden.shape
    blocks = units // BLOCK

    def copy_of(weight, buffer, sem, i):
        part = pl.ds(i * BLOCK, BLOCK)
        return pltpu.make_async_copy(weight.at[part], buffer.at[part], sem.at[i])

    for i in range(blocks):
        copy_of(gate_hbm, gate_buf, gate_sem, i).start()
        copy_of(up_hbm, up_buf, up_sem, i).start()
    for i in range(blocks):
        copy_of(down_hbm, down_buf, down_sem, i).start()

    for d in range(peers):
        wide[:, d * cols : (d + 1) * cols] = hidden[d].astype(F32)
    mean = jnp.sum(wide[...] * wide[...], axis=1, keepdims=True) * (1.0 / width)
    normed[...] = (wide[...] * lax.rsqrt(mean + EPS) * gain[...]).astype(BF16)
    expert = lax.axis_index("expert")
    own = own_rows.shape[0]
    mine = wide[0:own, :]
    for d in range(1, peers):
        mine = jnp.where(expert == d, wide[d * own : (d + 1) * own, :], mine)
    own_rows[...] = mine

    first_unit = (expert * lax.axis_size("tensor") + lax.axis_index("tensor")) * units
    lower = first_unit // FF
    boundary = (lower + 1) * FF - first_unit
    lane = lax.broadcasted_iota(jnp.int32, coefs.shape, 1)
    lower_coef = jnp.sum(jnp.where(lane == lower, coefs[...], 0.0), axis=1, keepdims=True)
    upper_coef = jnp.sum(jnp.where(lane == lower + 1, coefs[...], 0.0), axis=1, keepdims=True)
    dims = (((1,), (1,)), ((), ()))

    def unit_block(i, carry):
        copy_of(gate_hbm, gate_buf, gate_sem, i).wait()
        copy_of(up_hbm, up_buf, up_sem, i).wait()
        start = pl.multiple_of(i * BLOCK, BLOCK)
        part = pl.ds(start, BLOCK)
        gate = lax.dot_general(normed[...], gate_buf[part, :], dims, preferred_element_type=F32)
        up = lax.dot_general(normed[...], up_buf[part, :], dims, preferred_element_type=F32)
        column = lax.broadcasted_iota(jnp.int32, (rows, BLOCK), 1) + start
        coef = jnp.where(column < boundary, lower_coef, upper_coef)
        units_out[:, part] = (gate * jax.nn.sigmoid(gate) * up * coef).astype(BF16)
        return carry

    lax.fori_loop(0, blocks, unit_block, 0)
    total[...] = jnp.zeros_like(total)

    def down_block(i, carry):
        copy_of(down_hbm, down_buf, down_sem, i).wait()
        part = pl.ds(pl.multiple_of(i * BLOCK, BLOCK), BLOCK)
        total[...] += jnp.dot(units_out[:, part], down_buf[part, :], preferred_element_type=F32)
        return carry

    lax.fori_loop(0, blocks, down_block, 0)
    pieces, piece_rows, piece_cols = partial.shape
    across = width // piece_cols
    for p in range(pieces):
        r, c = p // across, p % across
        partial[p] = total[
            r * piece_rows : (r + 1) * piece_rows, c * piece_cols : (c + 1) * piece_cols
        ]


def sum_kernel(pieces, own_rows, out):
    half = out.shape[1]
    total = jnp.sum(pieces[...], axis=0)
    start = pl.multiple_of(lax.axis_index("tensor") * half, half)
    out[...] = (own_rows[:, pl.ds(start, half)] + total).astype(BF16)


def fused(
    conv_input,
    gate_input,
    step_input,
    b_proj,
    c_proj,
    slot_ids,
    state_pool,
    conv_pool,
    conv_weight,
    conv_bias,
    step_bias,
    a_log,
    d_skip,
    out_weight,
    residual,
    norm_gain,
    expert_ids,
    expert_probs,
    gate_weight,
    up_weight,
    down_weight,
):
    rows, channels = conv_input.shape
    width = residual.shape[1]
    units = gate_weight.shape[0]
    cols = out_weight.shape[1]
    peers = lax.axis_size("expert")
    halves = lax.axis_size("tensor")
    all_rows = peers * rows
    shape = jax.ShapeDtypeStruct
    packet_width = channels + cols + LANES

    new_state, packet = pl.pallas_call(
        mixer_kernel,
        out_shape=(
            shape((rows,) + state_pool.shape[1:], BF16),
            shape((peers, rows, packet_width), BF16),
        ),
        in_specs=[SMEM, SMEM] + [VMEM] * 13 + [SMEM],
        out_specs=(VMEM, VMEM),
        name="mixer",
    )(
        slot_ids,
        expert_ids,
        conv_input,
        gate_input,
        step_input,
        b_proj,
        c_proj,
        state_pool,
        jnp.transpose(conv_pool, (1, 0, 2)),
        conv_weight,
        conv_bias[None],
        step_bias[None],
        a_log,
        d_skip[None],
        residual,
        expert_probs.astype(F32),
    )
    packets = lax.all_to_all(packet, "expert", split_axis=0, concat_axis=0, tiled=True)
    partial_mixed, residual_block, coefs = pl.pallas_call(
        project_kernel,
        out_shape=(
            shape((all_rows, cols), F32),
            shape((all_rows, cols), F32),
            shape((all_rows, LANES), F32),
        ),
        in_specs=[VMEM] * 2,
        out_specs=(VMEM,) * 3,
        scratch_shapes=[pltpu.VMEM((all_rows, packet_width), F32)],
        name="project",
    )(packets, out_weight)
    swap = [(i, halves - 1 - i) for i in range(halves)]
    other_mixed = lax.ppermute(partial_mixed, "tensor", swap)
    hidden_copies = pl.pallas_call(
        hidden_kernel,
        out_shape=shape((peers, all_rows, cols), BF16),
        in_specs=[VMEM] * 3,
        out_specs=VMEM,
        name="hidden",
    )(partial_mixed, other_mixed, residual_block)
    hidden = lax.all_to_all(hidden_copies, "expert", split_axis=0, concat_axis=0, tiled=True)
    blocks = units // BLOCK
    partial_out, own_rows = pl.pallas_call(
        expert_kernel,
        out_shape=(
            shape((peers * halves, rows, width // halves), F32),
            shape((rows, width), F32),
        ),
        in_specs=[VMEM] * 3 + [ANY] * 3,
        out_specs=(VMEM, VMEM),
        scratch_shapes=[
            pltpu.VMEM((units, width), BF16),
            pltpu.VMEM((units, width), BF16),
            pltpu.VMEM((units, width), BF16),
            pltpu.VMEM((all_rows, width), F32),
            pltpu.VMEM((all_rows, width), BF16),
            pltpu.VMEM((all_rows, units), BF16),
            pltpu.VMEM((all_rows, width), F32),
            pltpu.SemaphoreType.DMA((blocks,)),
            pltpu.SemaphoreType.DMA((blocks,)),
            pltpu.SemaphoreType.DMA((blocks,)),
        ],
        compiler_params=pltpu.CompilerParams(vmem_limit_bytes=60 * 2**20),
        name="experts",
    )(hidden, coefs, norm_gain[None], gate_weight, up_weight, down_weight)
    pieces = lax.all_to_all(
        partial_out, ("expert", "tensor"), split_axis=0, concat_axis=0, tiled=True
    )
    half_out = pl.pallas_call(
        sum_kernel,
        out_shape=shape((rows, width // halves), BF16),
        in_specs=[VMEM] * 2,
        out_specs=VMEM,
        name="sum",
    )(pieces, own_rows)
    other_half = lax.ppermute(half_out, "tensor", swap)
    first = lax.axis_index("tensor") == 0
    layer_out = jnp.concatenate(
        [jnp.where(first, half_out, other_half), jnp.where(first, other_half, half_out)], axis=1
    )
    return (layer_out, new_state)


def body(*args):
    out_weight, gate_weight = args[13], args[18]
    tiled = (
        out_weight.shape[1] % LANES == 0
        and gate_weight.shape[0] % BLOCK == 0
        and lax.axis_size("tensor") == 2
    )
    return fused(*args) if tiled else local(*args)


def solution(mesh):
    return jax.shard_map(
        body,
        mesh=mesh,
        in_specs=(
            P(("groups", "expert"), "tensor"),
            P(("groups", "expert"), "tensor"),
            P(("groups", "expert"), "tensor"),
            P(("groups", "expert"), None),
            P(("groups", "expert"), None),
            P(("groups", "expert")),
            P(("groups", "expert"), None, "tensor"),
            P(("groups", "expert"), None, "tensor"),
            P(None, "tensor"),
            P("tensor"),
            P("tensor"),
            P(None, "tensor"),
            P("tensor"),
            P("tensor", "expert"),
            P(("groups", "expert"), None),
            P(),
            P(("groups", "expert"), None),
            P(("groups", "expert"), None),
            P(("expert", "tensor"), None),
            P(("expert", "tensor"), None),
            P(("expert", "tensor"), None),
        ),
        out_specs=(P(("groups", "expert"), None), P(("groups", "expert"), None, "tensor")),
        check_vma=False,
    )
```

```python
import jax
import jax.numpy as jnp
from jax import lax
from jax.experimental import pallas as pl
from jax.experimental.pallas import tpu as pltpu
from jax.sharding import PartitionSpec as P

EXPERTS = 3
FF = 12288


def mamba_step(
    states,
    history,
    conv_input,
    gate_input,
    step_input,
    b_proj,
    c_proj,
    conv_weight,
    conv_bias,
    step_bias,
    a_log,
    d_skip,
):
    inputs = conv_input.astype(jnp.float32)
    conv_sum = conv_weight[-1] * inputs + conv_bias
    for lag in range(history.shape[1]):
        conv_sum = conv_sum + conv_weight[lag] * history[:, lag]
    conv_out = jax.nn.silu(conv_sum)
    step_size = jax.nn.softplus(step_input.astype(jnp.float32) + step_bias)
    state_rates = -jnp.exp(a_log)
    decay_rate = jnp.exp(step_size[:, None, :] * state_rates[None])
    state_next = decay_rate * states + (step_size * conv_out)[:, None, :] * b_proj[:, :, None]
    output = jnp.sum(c_proj[:, :, None] * state_next, axis=1) + d_skip * conv_out
    gated_out = (output * jax.nn.silu(gate_input.astype(jnp.float32))).astype(jnp.bfloat16)
    return (state_next, gated_out)


def expert_terms(rows, coefs, first_unit, gate_weight, up_weight, down_weight):
    dims = (((1,), (1,)), ((), ()))
    gate_act = lax.dot_general(rows, gate_weight, dims, preferred_element_type=jnp.float32)
    up_act = lax.dot_general(rows, up_weight, dims, preferred_element_type=jnp.float32)
    hidden = (jax.nn.silu(gate_act) * up_act).astype(jnp.bfloat16)
    units = gate_weight.shape[0]
    lower_expert = first_unit // FF
    boundary = (lower_expert + 1) * FF - first_unit
    column = jnp.arange(units, dtype=jnp.int32)[None, :]
    zeros_bf = jnp.zeros_like(hidden)
    lower_hidden = jnp.where(column < boundary, hidden, zeros_bf)
    upper_hidden = jnp.where(column >= boundary, hidden, zeros_bf)
    expert_range = jnp.arange(EXPERTS, dtype=jnp.int32)[None, :]
    wide_coefs = coefs.astype(jnp.float32)
    lower_coef = jnp.sum(wide_coefs * (expert_range == lower_expert).astype(jnp.float32), axis=1)
    upper_coef = jnp.sum(
        wide_coefs * (expert_range == lower_expert + 1).astype(jnp.float32), axis=1
    )
    lower_out = jnp.dot(lower_hidden, down_weight, preferred_element_type=jnp.float32)
    upper_out = jnp.dot(upper_hidden, down_weight, preferred_element_type=jnp.float32)
    return lower_coef[:, None] * lower_out + upper_coef[:, None] * upper_out


def local(
    conv_input,
    gate_input,
    step_input,
    b_proj,
    c_proj,
    slot_ids,
    state_pool,
    conv_pool,
    conv_weight,
    conv_bias,
    step_bias,
    a_log,
    d_skip,
    out_weight,
    residual,
    norm_gain,
    expert_ids,
    expert_probs,
    gate_weight,
    up_weight,
    down_weight,
):
    pool_dev = state_pool.shape[0]
    local_slot = slot_ids - lax.axis_index("expert") * pool_dev
    select = (local_slot[:, None] == jnp.arange(pool_dev, dtype=jnp.int32)[None, :]).astype(
        jnp.bfloat16
    )
    states = jnp.einsum("rp,pnc->rnc", select, state_pool, preferred_element_type=jnp.float32)
    history = jnp.einsum("rp,pkc->rkc", select, conv_pool, preferred_element_type=jnp.float32)
    state_next, gated_out = mamba_step(
        states,
        history,
        conv_input,
        gate_input,
        step_input,
        b_proj,
        c_proj,
        conv_weight,
        conv_bias,
        step_bias,
        a_log,
        d_skip,
    )
    columns = jnp.dot(
        lax.all_gather(gated_out, "expert", axis=0, tiled=True),
        out_weight,
        preferred_element_type=jnp.float32,
    )
    returned_cols = lax.all_to_all(columns, "expert", split_axis=0, concat_axis=1, tiled=True)
    mixed = lax.psum(returned_cols, "tensor").astype(jnp.bfloat16)
    hidden_state = (residual.astype(jnp.float32) + mixed.astype(jnp.float32)).astype(jnp.bfloat16)
    wide = hidden_state.astype(jnp.float32)
    normed = (
        wide * lax.rsqrt(jnp.mean(wide * wide, axis=1, keepdims=True) + 1e-05) * norm_gain
    ).astype(jnp.bfloat16)
    probs = expert_probs.astype(jnp.float32)
    expert_range = jnp.arange(EXPERTS, dtype=jnp.int32)
    picked = (expert_ids[:, :, None] == expert_range[None, None, :]).astype(jnp.float32)
    coefs = jnp.sum(picked * probs[:, :, None], axis=1).astype(jnp.bfloat16)
    units = gate_weight.shape[0]
    first_unit = (
        lax.axis_index("expert") * lax.axis_size("tensor") + lax.axis_index("tensor")
    ) * units
    peers = lax.axis_size("expert")
    span = EXPERTS * FF // peers
    dest = jnp.arange(peers, dtype=jnp.int32)[:, None]
    intersection = (
        (expert_range[None, :] * FF < (dest + 1) * span)
        & ((expert_range[None, :] + 1) * FF > dest * span)
    ).astype(jnp.float32)
    chosen = jnp.sum(picked, axis=1)
    needed = jnp.dot(intersection, chosen.T, preferred_element_type=jnp.float32) > 0.5
    outgoing = jnp.where(needed[:, :, None], normed[None], jnp.zeros_like(normed)[None])
    out_coefs = jnp.broadcast_to(coefs[None], (peers, coefs.shape[0], coefs.shape[1]))
    rows_in = lax.all_to_all(outgoing, "expert", split_axis=0, concat_axis=0, tiled=True)
    coefs_in = lax.all_to_all(out_coefs, "expert", split_axis=0, concat_axis=0, tiled=True)
    flat_rows = rows_in.reshape(-1, rows_in.shape[2])
    flat_coefs = coefs_in.reshape(-1, coefs_in.shape[2])
    result = expert_terms(flat_rows, flat_coefs, first_unit, gate_weight, up_weight, down_weight)
    partial_value = result.reshape(rows_in.shape[0], rows_in.shape[1], rows_in.shape[2])
    returned = lax.all_to_all(partial_value, "expert", split_axis=0, concat_axis=0, tiled=True)
    routed = lax.psum(jnp.sum(returned, axis=0), "tensor")
    layer_out = (hidden_state.astype(jnp.float32) + routed).astype(jnp.bfloat16)
    return (layer_out, state_next.astype(jnp.bfloat16))


LANES = 128
BLOCK = 768
CHUNK = 384
SLOTS = 5
EPS = 1e-05
VMEM = pl.BlockSpec(memory_space=pltpu.VMEM)
SMEM = pl.BlockSpec(memory_space=pltpu.SMEM)
ANY = pl.BlockSpec(memory_space=pl.ANY)


def beside(bytes_accessed):
    return pl.CostEstimate(flops=bytes_accessed * 300, bytes_accessed=bytes_accessed, transcendentals=0)


F32 = jnp.float32
BF16 = jnp.bfloat16


def lane_to_sublane(row):
    n = row.shape[1]
    spread = jnp.broadcast_to(row, (n, n))
    diagonal = lax.broadcasted_iota(jnp.int32, (n, n), 0) == lax.broadcasted_iota(
        jnp.int32, (n, n), 1
    )
    return jnp.sum(jnp.where(diagonal, spread, 0.0), axis=1, keepdims=True)


def mixer_kernel(*refs):
    sources, (new_state, packet) = refs[:16], refs[16:18]
    buffers, sems = refs[18:34], refs[34]
    copies = [
        pltpu.make_async_copy(source, buffer, sems.at[i])
        for i, (source, buffer) in enumerate(zip(sources, buffers))
    ]
    for copy in copies:
        copy.start()
    for copy in copies:
        copy.wait()
    (
        slot_ref,
        ids_ref,
        conv_input,
        gate_input,
        step_input,
        b_proj,
        c_proj,
        state_pool,
        conv_pool,
        conv_weight,
        conv_bias,
        step_bias,
        a_log,
        d_skip,
        residual,
        probs,
    ) = buffers
    rows, channels = conv_input.shape
    peers = packet.shape[0]
    cols = residual.shape[1] // peers
    first_slot = lax.axis_index("expert") * state_pool.shape[0]
    rates = -jnp.exp(a_log[...])
    lane = lax.broadcasted_iota(jnp.int32, (1, LANES), 1)
    row = lax.broadcasted_iota(jnp.int32, (rows, channels), 0)
    slots = [slot_ref[r] - first_slot for r in range(rows)]
    conv = conv_weight[-1:, :] * conv_input[...].astype(F32) + conv_bias[...]
    for lag in range(conv_pool.shape[0]):
        past = conv_pool[lag].astype(F32)
        history = jnp.zeros((rows, channels), F32)
        for r in range(rows):
            for p in range(past.shape[0]):
                taken = (row == r) & (slots[r] == p)
                history = jnp.where(taken, past[p : p + 1, :], history)
        conv = conv + conv_weight[lag : lag + 1, :] * history
    conv_outs = conv * jax.nn.sigmoid(conv)
    steps = jax.nn.softplus(step_input[...].astype(F32) + step_bias[...])
    drives = steps * conv_outs
    gates = gate_input[...].astype(F32)
    gates = gates * jax.nn.sigmoid(gates)
    skips = d_skip[...] * conv_outs
    for r in range(rows):
        b = lane_to_sublane(b_proj[r : r + 1, :])
        c = lane_to_sublane(c_proj[r : r + 1, :])
        past = state_pool[slots[r]].astype(F32)
        state = jnp.exp(steps[r : r + 1, :] * rates) * past + drives[r : r + 1, :] * b
        new_state[r] = state.astype(BF16)
        output = jnp.sum(c * state, axis=0, keepdims=True) + skips[r : r + 1, :]
        gated = (output * gates[r : r + 1, :]).astype(BF16)
        coefs = jnp.zeros((1, LANES), F32)
        prob = probs[r : r + 1, :].astype(F32)
        for k in range(ids_ref.shape[1]):
            coefs = coefs + jnp.where(lane == ids_ref[r, k], prob[:, k : k + 1], 0.0)
        coefs = coefs.astype(BF16)
        for d in range(peers):
            packet[d, r : r + 1, 0:channels] = gated
            packet[d, r : r + 1, channels : channels + cols] = residual[
                r : r + 1, d * cols : (d + 1) * cols
            ]
            packet[d, r : r + 1, channels + cols :] = coefs


def project_kernel(packets, out_weight, partial, residual_block, coefs, rows_scratch):
    peers, rows, _ = packets.shape
    channels, cols = out_weight.shape
    for d in range(peers):
        rows_scratch[d * rows : (d + 1) * rows, :] = packets[d].astype(F32)
    partial[...] = jnp.dot(
        rows_scratch[:, 0:channels].astype(BF16), out_weight[...], preferred_element_type=F32
    )
    residual_block[...] = rows_scratch[:, channels : channels + cols]
    coefs[...] = rows_scratch[:, channels + cols :]


def hidden_kernel(mine, other, residual_block, copies):
    mixed = (mine[...] + other[...]).astype(BF16).astype(F32)
    hidden = (residual_block[...] + mixed).astype(BF16)
    for d in range(copies.shape[0]):
        copies[d] = hidden


def expert_kernel(
    hidden,
    coefs,
    gain,
    gate_weight,
    up_weight,
    down_hbm,
    partial,
    own_rows,
    down_buf,
    wide,
    normed,
    units_out,
    total,
    down_sem,
):
    units, width = gate_weight.shape
    peers, rows, cols = hidden.shape
    blocks = units // BLOCK

    chunks = units // CHUNK
    slots = down_buf.shape[0] // CHUNK

    def down_copy(i):
        slot = i % slots
        return pltpu.make_async_copy(
            down_hbm.at[pl.ds(i * CHUNK, CHUNK)],
            down_buf.at[pl.ds(slot * CHUNK, CHUNK)],
            down_sem.at[slot],
        )

    for i in range(slots):
        down_copy(i).start()

    for d in range(peers):
        wide[:, d * cols : (d + 1) * cols] = hidden[d].astype(F32)
    mean = jnp.sum(wide[...] * wide[...], axis=1, keepdims=True) * (1.0 / width)
    normed[...] = (wide[...] * lax.rsqrt(mean + EPS) * gain[...]).astype(BF16)
    expert = lax.axis_index("expert")
    own = own_rows.shape[0]
    mine = wide[0:own, :]
    for d in range(1, peers):
        mine = jnp.where(expert == d, wide[d * own : (d + 1) * own, :], mine)
    own_rows[...] = mine

    first_unit = (expert * lax.axis_size("tensor") + lax.axis_index("tensor")) * units
    lower = first_unit // FF
    boundary = (lower + 1) * FF - first_unit
    lane = lax.broadcasted_iota(jnp.int32, coefs.shape, 1)
    lower_coef = jnp.sum(jnp.where(lane == lower, coefs[...], 0.0), axis=1, keepdims=True)
    upper_coef = jnp.sum(jnp.where(lane == lower + 1, coefs[...], 0.0), axis=1, keepdims=True)
    dims = (((1,), (1,)), ((), ()))

    def unit_block(i, carry):
        start = pl.multiple_of(i * BLOCK, BLOCK)
        part = pl.ds(start, BLOCK)
        gate = lax.dot_general(normed[...], gate_weight[part, :], dims, preferred_element_type=F32)
        up = lax.dot_general(normed[...], up_weight[part, :], dims, preferred_element_type=F32)
        column = lax.broadcasted_iota(jnp.int32, (rows, BLOCK), 1) + start
        coef = jnp.where(column < boundary, lower_coef, upper_coef)
        units_out[:, part] = (gate * jax.nn.sigmoid(gate) * up * coef).astype(BF16)
        return carry

    lax.fori_loop(0, blocks, unit_block, 0)
    first = 0
    while first < chunks:
        slot = first % slots
        count = min(BLOCK // CHUNK, chunks - first, slots - slot)
        for i in range(first, first + count):
            down_copy(i).wait()
        product = jnp.dot(
            units_out[:, first * CHUNK : (first + count) * CHUNK],
            down_buf[slot * CHUNK : (slot + count) * CHUNK, :],
            preferred_element_type=F32,
        )
        total[...] = product if first == 0 else total[...] + product
        for i in range(first + slots, min(first + count + slots, chunks)):
            down_copy(i).start()
        first += count

    for d in range(peers):
        partial[d] = total[d * own : (d + 1) * own, :].astype(BF16)


def sum_kernel(pieces, out):
    total = pieces[0].astype(F32)
    for d in range(1, pieces.shape[0]):
        total = total + pieces[d].astype(F32)
    out[...] = total


def output_kernel(mine, other, own_rows, out):
    out[...] = (own_rows[...] + (mine[...] + other[...])).astype(BF16)


def run_experts(hidden, coefs, norm_gain, gate_weight, up_weight, down_weight):
    peers, all_rows, cols = hidden.shape
    units, width = gate_weight.shape
    rows = all_rows // peers
    shape = jax.ShapeDtypeStruct
    return pl.pallas_call(
        expert_kernel,
        out_shape=(
            shape((peers, rows, width), BF16),
            shape((rows, width), F32),
        ),
        in_specs=[VMEM] * 5 + [ANY],
        out_specs=(VMEM, VMEM),
        scratch_shapes=[
            pltpu.VMEM((SLOTS * CHUNK, width), BF16),
            pltpu.VMEM((all_rows, width), F32),
            pltpu.VMEM((all_rows, width), BF16),
            pltpu.VMEM((all_rows, units), BF16),
            pltpu.VMEM((all_rows, width), F32),
            pltpu.SemaphoreType.DMA((SLOTS,)),
        ],
        compiler_params=pltpu.CompilerParams(vmem_limit_bytes=17 * 2**20),
        name="experts",
    )(
        hidden,
        coefs,
        norm_gain[None],
        pltpu.with_memory_space_constraint(gate_weight, pltpu.VMEM),
        pltpu.with_memory_space_constraint(up_weight, pltpu.VMEM),
        down_weight,
    )


def fused(
    conv_input,
    gate_input,
    step_input,
    b_proj,
    c_proj,
    slot_ids,
    state_pool,
    conv_pool,
    conv_weight,
    conv_bias,
    step_bias,
    a_log,
    d_skip,
    out_weight,
    residual,
    norm_gain,
    expert_ids,
    expert_probs,
    gate_weight,
    up_weight,
    down_weight,
):
    rows, channels = conv_input.shape
    width = residual.shape[1]
    units = gate_weight.shape[0]
    cols = out_weight.shape[1]
    peers = lax.axis_size("expert")
    halves = lax.axis_size("tensor")
    all_rows = peers * rows
    shape = jax.ShapeDtypeStruct
    packet_width = channels + cols + LANES

    mixer_inputs = (
        slot_ids,
        expert_ids,
        conv_input,
        gate_input,
        step_input,
        b_proj,
        c_proj,
        state_pool,
        jnp.transpose(conv_pool, (1, 0, 2)),
        conv_weight,
        conv_bias[None],
        step_bias[None],
        a_log,
        d_skip[None],
        residual,
        expert_probs,
    )
    new_state, packet = pl.pallas_call(
        mixer_kernel,
        out_shape=(
            shape((rows,) + state_pool.shape[1:], BF16),
            shape((peers, rows, packet_width), BF16),
        ),
        in_specs=[ANY] * len(mixer_inputs),
        out_specs=(VMEM, VMEM),
        scratch_shapes=[pltpu.SMEM(x.shape, x.dtype) for x in mixer_inputs[:2]]
        + [pltpu.VMEM(x.shape, x.dtype) for x in mixer_inputs[2:]]
        + [pltpu.SemaphoreType.DMA((len(mixer_inputs),))],
        compiler_params=pltpu.CompilerParams(vmem_limit_bytes=6 * 2**20),
        cost_estimate=beside(300000000),
        name="mixer",
    )(*(pltpu.with_memory_space_constraint(x, pltpu.HBM) for x in mixer_inputs))
    packets = lax.all_to_all(packet, "expert", split_axis=0, concat_axis=0, tiled=True)
    partial_mixed, residual_block, coefs = pl.pallas_call(
        project_kernel,
        out_shape=(
            shape((all_rows, cols), F32),
            shape((all_rows, cols), F32),
            shape((all_rows, LANES), F32),
        ),
        in_specs=[VMEM] * 2,
        out_specs=(VMEM,) * 3,
        scratch_shapes=[pltpu.VMEM((all_rows, packet_width), F32)],
        compiler_params=pltpu.CompilerParams(vmem_limit_bytes=6 * 2**20),
        cost_estimate=beside(300000000),
        name="project",
    )(packets, out_weight)
    swap = [(i, halves - 1 - i) for i in range(halves)]
    other_mixed = lax.ppermute(partial_mixed, "tensor", swap)
    hidden_copies = pl.pallas_call(
        hidden_kernel,
        out_shape=shape((peers, all_rows, cols), BF16),
        in_specs=[VMEM] * 3,
        out_specs=VMEM,
        compiler_params=pltpu.CompilerParams(vmem_limit_bytes=2 * 2**20),
        cost_estimate=beside(150000000),
        name="hidden",
    )(partial_mixed, other_mixed, residual_block)
    hidden = lax.all_to_all(hidden_copies, "expert", split_axis=0, concat_axis=0, tiled=True)
    partial_out, own_rows = run_experts(
        hidden, coefs, norm_gain, gate_weight, up_weight, down_weight
    )
    pieces = lax.all_to_all(partial_out, "expert", split_axis=0, concat_axis=0, tiled=True)
    routed = pl.pallas_call(
        sum_kernel,
        out_shape=shape((rows, width), F32),
        in_specs=[VMEM],
        out_specs=VMEM,
        compiler_params=pltpu.CompilerParams(vmem_limit_bytes=2 * 2**20),
        name="sum",
    )(pieces)
    other_routed = lax.ppermute(routed, "tensor", swap)
    layer_out = pl.pallas_call(
        output_kernel,
        out_shape=shape((rows, width), BF16),
        in_specs=[VMEM] * 3,
        out_specs=VMEM,
        compiler_params=pltpu.CompilerParams(vmem_limit_bytes=2 * 2**20),
        name="output",
    )(routed, other_routed, own_rows)
    return (layer_out, new_state)


def body(*args):
    out_weight, gate_weight = args[13], args[18]
    tiled = (
        out_weight.shape[1] % LANES == 0
        and gate_weight.shape[0] % BLOCK == 0
        and lax.axis_size("tensor") == 2
    )
    return fused(*args) if tiled else local(*args)


def solution(mesh):
    return jax.shard_map(
        body,
        mesh=mesh,
        in_specs=(
            P(("groups", "expert"), "tensor"),
            P(("groups", "expert"), "tensor"),
            P(("groups", "expert"), "tensor"),
            P(("groups", "expert"), None),
            P(("groups", "expert"), None),
            P(("groups", "expert")),
            P(("groups", "expert"), None, "tensor"),
            P(("groups", "expert"), None, "tensor"),
            P(None, "tensor"),
            P("tensor"),
            P("tensor"),
            P(None, "tensor"),
            P("tensor"),
            P("tensor", "expert"),
            P(("groups", "expert"), None),
            P(),
            P(("groups", "expert"), None),
            P(("groups", "expert"), None),
            P(("expert", "tensor"), None),
            P(("expert", "tensor"), None),
            P(("expert", "tensor"), None),
        ),
        out_specs=(P(("groups", "expert"), None), P(("groups", "expert"), None, "tensor")),
        check_vma=False,
    )
```

```python
import jax
import jax.numpy as jnp
from jax import lax
from jax.experimental import pallas as pl
from jax.experimental.pallas import tpu as pltpu
from jax.sharding import PartitionSpec as P

EXPERTS = 3
FF = 12288


def mamba_step(
    states,
    history,
    conv_input,
    gate_input,
    step_input,
    b_proj,
    c_proj,
    conv_weight,
    conv_bias,
    step_bias,
    a_log,
    d_skip,
):
    inputs = conv_input.astype(jnp.float32)
    conv_sum = conv_weight[-1] * inputs + conv_bias
    for lag in range(history.shape[1]):
        conv_sum = conv_sum + conv_weight[lag] * history[:, lag]
    conv_out = jax.nn.silu(conv_sum)
    step_size = jax.nn.softplus(step_input.astype(jnp.float32) + step_bias)
    state_rates = -jnp.exp(a_log)
    decay_rate = jnp.exp(step_size[:, None, :] * state_rates[None])
    state_next = decay_rate * states + (step_size * conv_out)[:, None, :] * b_proj[:, :, None]
    output = jnp.sum(c_proj[:, :, None] * state_next, axis=1) + d_skip * conv_out
    gated_out = (output * jax.nn.silu(gate_input.astype(jnp.float32))).astype(jnp.bfloat16)
    return (state_next, gated_out)


def expert_terms(rows, coefs, first_unit, gate_weight, up_weight, down_weight):
    dims = (((1,), (1,)), ((), ()))
    gate_act = lax.dot_general(rows, gate_weight, dims, preferred_element_type=jnp.float32)
    up_act = lax.dot_general(rows, up_weight, dims, preferred_element_type=jnp.float32)
    hidden = (jax.nn.silu(gate_act) * up_act).astype(jnp.bfloat16)
    units = gate_weight.shape[0]
    lower_expert = first_unit // FF
    boundary = (lower_expert + 1) * FF - first_unit
    column = jnp.arange(units, dtype=jnp.int32)[None, :]
    zeros_bf = jnp.zeros_like(hidden)
    lower_hidden = jnp.where(column < boundary, hidden, zeros_bf)
    upper_hidden = jnp.where(column >= boundary, hidden, zeros_bf)
    expert_range = jnp.arange(EXPERTS, dtype=jnp.int32)[None, :]
    wide_coefs = coefs.astype(jnp.float32)
    lower_coef = jnp.sum(wide_coefs * (expert_range == lower_expert).astype(jnp.float32), axis=1)
    upper_coef = jnp.sum(
        wide_coefs * (expert_range == lower_expert + 1).astype(jnp.float32), axis=1
    )
    lower_out = jnp.dot(lower_hidden, down_weight, preferred_element_type=jnp.float32)
    upper_out = jnp.dot(upper_hidden, down_weight, preferred_element_type=jnp.float32)
    return lower_coef[:, None] * lower_out + upper_coef[:, None] * upper_out


def local(
    conv_input,
    gate_input,
    step_input,
    b_proj,
    c_proj,
    slot_ids,
    state_pool,
    conv_pool,
    conv_weight,
    conv_bias,
    step_bias,
    a_log,
    d_skip,
    out_weight,
    residual,
    norm_gain,
    expert_ids,
    expert_probs,
    gate_weight,
    up_weight,
    down_weight,
):
    pool_dev = state_pool.shape[0]
    local_slot = slot_ids - lax.axis_index("expert") * pool_dev
    select = (local_slot[:, None] == jnp.arange(pool_dev, dtype=jnp.int32)[None, :]).astype(
        jnp.bfloat16
    )
    states = jnp.einsum("rp,pnc->rnc", select, state_pool, preferred_element_type=jnp.float32)
    history = jnp.einsum("rp,pkc->rkc", select, conv_pool, preferred_element_type=jnp.float32)
    state_next, gated_out = mamba_step(
        states,
        history,
        conv_input,
        gate_input,
        step_input,
        b_proj,
        c_proj,
        conv_weight,
        conv_bias,
        step_bias,
        a_log,
        d_skip,
    )
    columns = jnp.dot(
        lax.all_gather(gated_out, "expert", axis=0, tiled=True),
        out_weight,
        preferred_element_type=jnp.float32,
    )
    returned_cols = lax.all_to_all(columns, "expert", split_axis=0, concat_axis=1, tiled=True)
    mixed = lax.psum(returned_cols, "tensor").astype(jnp.bfloat16)
    hidden_state = (residual.astype(jnp.float32) + mixed.astype(jnp.float32)).astype(jnp.bfloat16)
    wide = hidden_state.astype(jnp.float32)
    normed = (
        wide * lax.rsqrt(jnp.mean(wide * wide, axis=1, keepdims=True) + 1e-05) * norm_gain
    ).astype(jnp.bfloat16)
    probs = expert_probs.astype(jnp.float32)
    expert_range = jnp.arange(EXPERTS, dtype=jnp.int32)
    picked = (expert_ids[:, :, None] == expert_range[None, None, :]).astype(jnp.float32)
    coefs = jnp.sum(picked * probs[:, :, None], axis=1).astype(jnp.bfloat16)
    units = gate_weight.shape[0]
    first_unit = (
        lax.axis_index("expert") * lax.axis_size("tensor") + lax.axis_index("tensor")
    ) * units
    peers = lax.axis_size("expert")
    span = EXPERTS * FF // peers
    dest = jnp.arange(peers, dtype=jnp.int32)[:, None]
    intersection = (
        (expert_range[None, :] * FF < (dest + 1) * span)
        & ((expert_range[None, :] + 1) * FF > dest * span)
    ).astype(jnp.float32)
    chosen = jnp.sum(picked, axis=1)
    needed = jnp.dot(intersection, chosen.T, preferred_element_type=jnp.float32) > 0.5
    outgoing = jnp.where(needed[:, :, None], normed[None], jnp.zeros_like(normed)[None])
    out_coefs = jnp.broadcast_to(coefs[None], (peers, coefs.shape[0], coefs.shape[1]))
    rows_in = lax.all_to_all(outgoing, "expert", split_axis=0, concat_axis=0, tiled=True)
    coefs_in = lax.all_to_all(out_coefs, "expert", split_axis=0, concat_axis=0, tiled=True)
    flat_rows = rows_in.reshape(-1, rows_in.shape[2])
    flat_coefs = coefs_in.reshape(-1, coefs_in.shape[2])
    result = expert_terms(flat_rows, flat_coefs, first_unit, gate_weight, up_weight, down_weight)
    partial_value = result.reshape(rows_in.shape[0], rows_in.shape[1], rows_in.shape[2])
    returned = lax.all_to_all(partial_value, "expert", split_axis=0, concat_axis=0, tiled=True)
    routed = lax.psum(jnp.sum(returned, axis=0), "tensor")
    layer_out = (hidden_state.astype(jnp.float32) + routed).astype(jnp.bfloat16)
    return (layer_out, state_next.astype(jnp.bfloat16))


LANES = 128
BLOCK = 256
SLOTS = 5
EPS = 1e-05
VMEM = pl.BlockSpec(memory_space=pltpu.VMEM)
SMEM = pl.BlockSpec(memory_space=pltpu.SMEM)
ANY = pl.BlockSpec(memory_space=pl.ANY)


def beside(bytes_accessed):
    return pl.CostEstimate(flops=bytes_accessed * 300, bytes_accessed=bytes_accessed, transcendentals=0)


F32 = jnp.float32
BF16 = jnp.bfloat16


def lane_to_sublane(row):
    n = row.shape[1]
    spread = jnp.broadcast_to(row, (n, n))
    diagonal = lax.broadcasted_iota(jnp.int32, (n, n), 0) == lax.broadcasted_iota(
        jnp.int32, (n, n), 1
    )
    return jnp.sum(jnp.where(diagonal, spread, 0.0), axis=1, keepdims=True)


def mixer_kernel(*refs):
    sources, (new_state, packet) = refs[:16], refs[16:18]
    buffers, sems = refs[18:34], refs[34]
    copies = [
        pltpu.make_async_copy(source, buffer, sems.at[i])
        for i, (source, buffer) in enumerate(zip(sources, buffers))
    ]
    for copy in copies:
        copy.start()
    late = (7, 12)
    for i, copy in enumerate(copies):
        if i not in late:
            copy.wait()
    (
        slot_ref,
        ids_ref,
        conv_input,
        gate_input,
        step_input,
        b_proj,
        c_proj,
        state_pool,
        conv_pool,
        conv_weight,
        conv_bias,
        step_bias,
        a_log,
        d_skip,
        residual,
        probs,
    ) = buffers
    rows, channels = conv_input.shape
    peers = packet.shape[0]
    cols = residual.shape[1] // peers
    first_slot = lax.axis_index("expert") * state_pool.shape[0]
    lane = lax.broadcasted_iota(jnp.int32, (1, LANES), 1)
    row = lax.broadcasted_iota(jnp.int32, (rows, channels), 0)
    slots = [slot_ref[r] - first_slot for r in range(rows)]
    conv = conv_weight[-1:, :] * conv_input[...].astype(F32) + conv_bias[...]
    for lag in range(conv_pool.shape[0]):
        past = conv_pool[lag].astype(F32)
        history = jnp.zeros((rows, channels), F32)
        for r in range(rows):
            for p in range(past.shape[0]):
                taken = (row == r) & (slots[r] == p)
                history = jnp.where(taken, past[p : p + 1, :], history)
        conv = conv + conv_weight[lag : lag + 1, :] * history
    conv_outs = conv * jax.nn.sigmoid(conv)
    steps = jax.nn.softplus(step_input[...].astype(F32) + step_bias[...])
    drives = steps * conv_outs
    gates = gate_input[...].astype(F32)
    gates = gates * jax.nn.sigmoid(gates)
    skips = d_skip[...] * conv_outs
    for i in late:
        copies[i].wait()
    rates = -jnp.exp(a_log[...])
    for r in range(rows):
        b = lane_to_sublane(b_proj[r : r + 1, :])
        c = lane_to_sublane(c_proj[r : r + 1, :])
        past = state_pool[slots[r]].astype(F32)
        state = jnp.exp(steps[r : r + 1, :] * rates) * past + drives[r : r + 1, :] * b
        new_state[r] = state.astype(BF16)
        output = jnp.sum(c * state, axis=0, keepdims=True) + skips[r : r + 1, :]
        gated = (output * gates[r : r + 1, :]).astype(BF16)
        coefs = jnp.zeros((1, LANES), F32)
        prob = probs[r : r + 1, :].astype(F32)
        for k in range(ids_ref.shape[1]):
            coefs = coefs + jnp.where(lane == ids_ref[r, k], prob[:, k : k + 1], 0.0)
        coefs = coefs.astype(BF16)
        for d in range(peers):
            packet[d, r : r + 1, 0:channels] = gated
            packet[d, r : r + 1, channels : channels + cols] = residual[
                r : r + 1, d * cols : (d + 1) * cols
            ]
            packet[d, r : r + 1, channels + cols :] = coefs


def project_kernel(packets, out_weight, partial, residual_block, coefs, rows_scratch):
    peers, rows, _ = packets.shape
    channels, cols = out_weight.shape
    for d in range(peers):
        rows_scratch[d * rows : (d + 1) * rows, :] = packets[d].astype(F32)
    partial[...] = jnp.dot(
        rows_scratch[:, 0:channels].astype(BF16), out_weight[...], preferred_element_type=F32
    )
    residual_block[...] = rows_scratch[:, channels : channels + cols]
    coefs[...] = rows_scratch[:, channels + cols :]


def hidden_kernel(mine, other, residual_block, copies):
    mixed = (mine[...] + other[...]).astype(BF16).astype(F32)
    hidden = (residual_block[...] + mixed).astype(BF16)
    for d in range(copies.shape[0]):
        copies[d] = hidden


def expert_kernel(
    hidden,
    coefs,
    gain,
    gate_weight,
    up_weight,
    down_hbm,
    partial,
    own_rows,
    turned,
    down_buf,
    wide,
    normed,
    units_out,
    down_sem,
):
    units, width = gate_weight.shape
    peers, rows, cols = hidden.shape
    blocks = units // BLOCK

    steps = units // BLOCK
    slots = down_buf.shape[0]

    def down_copy(step):
        slot = lax.rem(step, slots)
        rows = pl.ds(step * BLOCK, BLOCK)
        return pltpu.make_async_copy(down_hbm.at[rows], down_buf.at[slot], down_sem.at[slot])

    def start_copy(i, carry):
        down_copy(i).start()
        return carry

    lax.fori_loop(0, slots, start_copy, 0)
    half = BLOCK // 2

    def turn(step):
        part = pl.ds(step * BLOCK + half, half)
        turned[step % 2, :, 0:half] = gate_weight[part, :].T
        turned[step % 2, :, half:] = up_weight[part, :].T

    turn(0)
    for d in range(peers):
        wide[:, d * cols : (d + 1) * cols] = hidden[d].astype(F32)
    mean = jnp.sum(wide[...] * wide[...], axis=1, keepdims=True) * (1.0 / width)
    normed[...] = (wide[...] * lax.rsqrt(mean + EPS) * gain[...]).astype(BF16)
    expert = lax.axis_index("expert")
    own = own_rows.shape[0]
    mine = wide[0:own, :]
    for d in range(1, peers):
        mine = jnp.where(expert == d, wide[d * own : (d + 1) * own, :], mine)
    own_rows[...] = mine

    first_unit = (expert * lax.axis_size("tensor") + lax.axis_index("tensor")) * units
    lower = first_unit // FF
    boundary = (lower + 1) * FF - first_unit
    lane = lax.broadcasted_iota(jnp.int32, coefs.shape, 1)
    lower_coef = jnp.sum(jnp.where(lane == lower, coefs[...], 0.0), axis=1, keepdims=True)
    upper_coef = jnp.sum(jnp.where(lane == lower + 1, coefs[...], 0.0), axis=1, keepdims=True)
    dims = (((1,), (1,)), ((), ()))

    def finish(start, gate, up):
        column = lax.broadcasted_iota(jnp.int32, gate.shape, 1) + start
        coef = jnp.where(column < boundary, lower_coef, upper_coef)
        hidden_units = gate * jax.nn.sigmoid(gate) * up * coef
        units_out[:, start : start + gate.shape[1]] = hidden_units.astype(BF16)

    total = wide

    def unit_step(step):
        start = step * BLOCK
        if step + 1 < steps:
            turn(step + 1)
        part = pl.ds(start, half)
        gate = lax.dot_general(normed[...], gate_weight[part, :], dims, preferred_element_type=F32)
        up = lax.dot_general(normed[...], up_weight[part, :], dims, preferred_element_type=F32)
        finish(start, gate, up)
        both = jnp.dot(normed[...], turned[step % 2], preferred_element_type=F32)
        finish(start + half, both[:, 0:half], both[:, half:])

    def down_step(step):
        product = jnp.dot(
            units_out[:, step * BLOCK : (step + 1) * BLOCK],
            down_buf[step % slots],
            preferred_element_type=F32,
        )
        total[...] = product if step == 0 else total[...] + product

    for step in range(steps + 1):
        if step > 0:
            down_copy(step - 1).wait()

        @pl.when(lower >= 0)
        def _():
            if step > 0:
                down_step(step - 1)
            if step < steps:
                unit_step(step)

        if step > 0 and step - 1 + slots < steps:
            down_copy(step - 1 + slots).start()

    for d in range(peers):
        partial[d] = total[d * own : (d + 1) * own, :].astype(BF16)


def sum_kernel(pieces, out):
    total = pieces[0].astype(F32)
    for d in range(1, pieces.shape[0]):
        total = total + pieces[d].astype(F32)
    out[...] = total


def output_kernel(mine, other, own_rows, out):
    out[...] = (own_rows[...] + (mine[...] + other[...])).astype(BF16)


def run_experts(hidden, coefs, norm_gain, gate_weight, up_weight, down_weight):
    peers, all_rows, cols = hidden.shape
    units, width = gate_weight.shape
    rows = all_rows // peers
    shape = jax.ShapeDtypeStruct
    return pl.pallas_call(
        expert_kernel,
        out_shape=(
            shape((peers, rows, width), BF16),
            shape((rows, width), F32),
        ),
        in_specs=[VMEM] * 5 + [ANY],
        out_specs=(VMEM, VMEM),
        scratch_shapes=[
            pltpu.VMEM((2, width, BLOCK), BF16),
            pltpu.VMEM((SLOTS, BLOCK, width), BF16),
            pltpu.VMEM((all_rows, width), F32),
            pltpu.VMEM((all_rows, width), BF16),
            pltpu.VMEM((all_rows, units), BF16),
            pltpu.SemaphoreType.DMA((SLOTS,)),
        ],
        compiler_params=pltpu.CompilerParams(vmem_limit_bytes=16 * 2**20),
        name="experts",
    )(
        hidden,
        coefs,
        norm_gain[None],
        pltpu.with_memory_space_constraint(gate_weight, pltpu.VMEM),
        pltpu.with_memory_space_constraint(up_weight, pltpu.VMEM),
        down_weight,
    )


def run_mixer(peers, cols, conv_input, gate_input, step_input, b_proj, c_proj, slot_ids, state_pool, conv_pool, conv_weight, conv_bias, step_bias, a_log, d_skip, residual, expert_ids, expert_probs):
    rows, channels = conv_input.shape
    packet_width = channels + cols + LANES
    shape = jax.ShapeDtypeStruct
    mixer_inputs = (
        slot_ids,
        expert_ids,
        conv_input,
        gate_input,
        step_input,
        b_proj,
        c_proj,
        state_pool,
        jnp.transpose(conv_pool, (1, 0, 2)),
        conv_weight,
        conv_bias[None],
        step_bias[None],
        a_log,
        d_skip[None],
        residual,
        expert_probs,
    )
    return pl.pallas_call(
        mixer_kernel,
        out_shape=(
            pltpu.VMEM((rows,) + state_pool.shape[1:], BF16),
            shape((peers, rows, packet_width), BF16),
        ),
        in_specs=[ANY] * len(mixer_inputs),
        out_specs=(VMEM, VMEM),
        scratch_shapes=[pltpu.SMEM(x.shape, x.dtype) for x in mixer_inputs[:2]]
        + [pltpu.VMEM(x.shape, x.dtype) for x in mixer_inputs[2:]]
        + [pltpu.SemaphoreType.DMA((len(mixer_inputs),))],
        compiler_params=pltpu.CompilerParams(vmem_limit_bytes=6 * 2**20),
        cost_estimate=beside(300000000),
        name="mixer",
    )(*(pltpu.with_memory_space_constraint(x, pltpu.HBM) for x in mixer_inputs))


def fused(
    conv_input,
    gate_input,
    step_input,
    b_proj,
    c_proj,
    slot_ids,
    state_pool,
    conv_pool,
    conv_weight,
    conv_bias,
    step_bias,
    a_log,
    d_skip,
    out_weight,
    residual,
    norm_gain,
    expert_ids,
    expert_probs,
    gate_weight,
    up_weight,
    down_weight,
):
    rows, channels = conv_input.shape
    width = residual.shape[1]
    units = gate_weight.shape[0]
    cols = out_weight.shape[1]
    peers = lax.axis_size("expert")
    halves = lax.axis_size("tensor")
    all_rows = peers * rows
    shape = jax.ShapeDtypeStruct
    packet_width = channels + cols + LANES

    new_state, packet = run_mixer(
        peers,
        cols,
        conv_input,
        gate_input,
        step_input,
        b_proj,
        c_proj,
        slot_ids,
        state_pool,
        conv_pool,
        conv_weight,
        conv_bias,
        step_bias,
        a_log,
        d_skip,
        residual,
        expert_ids,
        expert_probs,
    )
    packets = lax.all_to_all(packet, "expert", split_axis=0, concat_axis=0, tiled=True)
    partial_mixed, residual_block, coefs = pl.pallas_call(
        project_kernel,
        out_shape=(
            shape((all_rows, cols), F32),
            shape((all_rows, cols), F32),
            shape((all_rows, LANES), F32),
        ),
        in_specs=[VMEM] * 2,
        out_specs=(VMEM,) * 3,
        scratch_shapes=[pltpu.VMEM((all_rows, packet_width), F32)],
        compiler_params=pltpu.CompilerParams(vmem_limit_bytes=6 * 2**20),
        cost_estimate=beside(300000000),
        name="project",
    )(packets, out_weight)
    swap = [(i, halves - 1 - i) for i in range(halves)]
    other_mixed = lax.ppermute(partial_mixed, "tensor", swap)
    hidden_copies = pl.pallas_call(
        hidden_kernel,
        out_shape=shape((peers, all_rows, cols), BF16),
        in_specs=[VMEM] * 3,
        out_specs=VMEM,
        compiler_params=pltpu.CompilerParams(vmem_limit_bytes=2 * 2**20),
        cost_estimate=beside(150000000),
        name="hidden",
    )(partial_mixed, other_mixed, residual_block)
    hidden = lax.all_to_all(hidden_copies, "expert", split_axis=0, concat_axis=0, tiled=True)
    partial_out, own_rows = run_experts(
        hidden, coefs, norm_gain, gate_weight, up_weight, down_weight
    )
    pieces = lax.all_to_all(partial_out, "expert", split_axis=0, concat_axis=0, tiled=True)
    routed = pl.pallas_call(
        sum_kernel,
        out_shape=shape((rows, width), F32),
        in_specs=[VMEM],
        out_specs=VMEM,
        compiler_params=pltpu.CompilerParams(vmem_limit_bytes=2 * 2**20),
        name="sum",
    )(pieces)
    other_routed = lax.ppermute(routed, "tensor", swap)
    layer_out = pl.pallas_call(
        output_kernel,
        out_shape=shape((rows, width), BF16),
        in_specs=[VMEM] * 3,
        out_specs=VMEM,
        compiler_params=pltpu.CompilerParams(vmem_limit_bytes=2 * 2**20),
        name="output",
    )(routed, other_routed, own_rows)
    return (layer_out, new_state)


def body(*args):
    out_weight, gate_weight = args[13], args[18]
    tiled = (
        out_weight.shape[1] % LANES == 0
        and gate_weight.shape[0] % BLOCK == 0
        and gate_weight.shape[0] // BLOCK >= SLOTS
        and lax.axis_size("tensor") == 2
    )
    return fused(*args) if tiled else local(*args)


def solution(mesh):
    return jax.shard_map(
        body,
        mesh=mesh,
        in_specs=(
            P(("groups", "expert"), "tensor"),
            P(("groups", "expert"), "tensor"),
            P(("groups", "expert"), "tensor"),
            P(("groups", "expert"), None),
            P(("groups", "expert"), None),
            P(("groups", "expert")),
            P(("groups", "expert"), None, "tensor"),
            P(("groups", "expert"), None, "tensor"),
            P(None, "tensor"),
            P("tensor"),
            P("tensor"),
            P(None, "tensor"),
            P("tensor"),
            P("tensor", "expert"),
            P(("groups", "expert"), None),
            P(),
            P(("groups", "expert"), None),
            P(("groups", "expert"), None),
            P(("expert", "tensor"), None),
            P(("expert", "tensor"), None),
            P(("expert", "tensor"), None),
        ),
        out_specs=(P(("groups", "expert"), None), P(("groups", "expert"), None, "tensor")),
        check_vma=False,
    )
```

```python
import jax
import jax.numpy as jnp
from jax import lax
from jax.experimental import pallas as pl
from jax.experimental.pallas import tpu as pltpu
from jax.sharding import PartitionSpec as P

EXPERTS = 3
FF = 12288


def mamba_step(
    states,
    history,
    conv_input,
    gate_input,
    step_input,
    b_proj,
    c_proj,
    conv_weight,
    conv_bias,
    step_bias,
    a_log,
    d_skip,
):
    inputs = conv_input.astype(jnp.float32)
    conv_sum = conv_weight[-1] * inputs + conv_bias
    for lag in range(history.shape[1]):
        conv_sum = conv_sum + conv_weight[lag] * history[:, lag]
    conv_out = jax.nn.silu(conv_sum)
    step_size = jax.nn.softplus(step_input.astype(jnp.float32) + step_bias)
    state_rates = -jnp.exp(a_log)
    decay_rate = jnp.exp(step_size[:, None, :] * state_rates[None])
    state_next = decay_rate * states + (step_size * conv_out)[:, None, :] * b_proj[:, :, None]
    output = jnp.sum(c_proj[:, :, None] * state_next, axis=1) + d_skip * conv_out
    gated_out = (output * jax.nn.silu(gate_input.astype(jnp.float32))).astype(jnp.bfloat16)
    return (state_next, gated_out)


def expert_terms(rows, coefs, first_unit, gate_weight, up_weight, down_weight):
    dims = (((1,), (1,)), ((), ()))
    gate_act = lax.dot_general(rows, gate_weight, dims, preferred_element_type=jnp.float32)
    up_act = lax.dot_general(rows, up_weight, dims, preferred_element_type=jnp.float32)
    hidden = (jax.nn.silu(gate_act) * up_act).astype(jnp.bfloat16)
    units = gate_weight.shape[0]
    lower_expert = first_unit // FF
    boundary = (lower_expert + 1) * FF - first_unit
    column = jnp.arange(units, dtype=jnp.int32)[None, :]
    zeros_bf = jnp.zeros_like(hidden)
    lower_hidden = jnp.where(column < boundary, hidden, zeros_bf)
    upper_hidden = jnp.where(column >= boundary, hidden, zeros_bf)
    expert_range = jnp.arange(EXPERTS, dtype=jnp.int32)[None, :]
    wide_coefs = coefs.astype(jnp.float32)
    lower_coef = jnp.sum(wide_coefs * (expert_range == lower_expert).astype(jnp.float32), axis=1)
    upper_coef = jnp.sum(
        wide_coefs * (expert_range == lower_expert + 1).astype(jnp.float32), axis=1
    )
    lower_out = jnp.dot(lower_hidden, down_weight, preferred_element_type=jnp.float32)
    upper_out = jnp.dot(upper_hidden, down_weight, preferred_element_type=jnp.float32)
    return lower_coef[:, None] * lower_out + upper_coef[:, None] * upper_out


def local(
    conv_input,
    gate_input,
    step_input,
    b_proj,
    c_proj,
    slot_ids,
    state_pool,
    conv_pool,
    conv_weight,
    conv_bias,
    step_bias,
    a_log,
    d_skip,
    out_weight,
    residual,
    norm_gain,
    expert_ids,
    expert_probs,
    gate_weight,
    up_weight,
    down_weight,
):
    pool_dev = state_pool.shape[0]
    local_slot = slot_ids - lax.axis_index("expert") * pool_dev
    select = (local_slot[:, None] == jnp.arange(pool_dev, dtype=jnp.int32)[None, :]).astype(
        jnp.bfloat16
    )
    states = jnp.einsum("rp,pnc->rnc", select, state_pool, preferred_element_type=jnp.float32)
    history = jnp.einsum("rp,pkc->rkc", select, conv_pool, preferred_element_type=jnp.float32)
    state_next, gated_out = mamba_step(
        states,
        history,
        conv_input,
        gate_input,
        step_input,
        b_proj,
        c_proj,
        conv_weight,
        conv_bias,
        step_bias,
        a_log,
        d_skip,
    )
    columns = jnp.dot(
        lax.all_gather(gated_out, "expert", axis=0, tiled=True),
        out_weight,
        preferred_element_type=jnp.float32,
    )
    returned_cols = lax.all_to_all(columns, "expert", split_axis=0, concat_axis=1, tiled=True)
    mixed = lax.psum(returned_cols, "tensor").astype(jnp.bfloat16)
    hidden_state = (residual.astype(jnp.float32) + mixed.astype(jnp.float32)).astype(jnp.bfloat16)
    wide = hidden_state.astype(jnp.float32)
    normed = (
        wide * lax.rsqrt(jnp.mean(wide * wide, axis=1, keepdims=True) + 1e-05) * norm_gain
    ).astype(jnp.bfloat16)
    probs = expert_probs.astype(jnp.float32)
    expert_range = jnp.arange(EXPERTS, dtype=jnp.int32)
    picked = (expert_ids[:, :, None] == expert_range[None, None, :]).astype(jnp.float32)
    coefs = jnp.sum(picked * probs[:, :, None], axis=1).astype(jnp.bfloat16)
    units = gate_weight.shape[0]
    first_unit = (
        lax.axis_index("expert") * lax.axis_size("tensor") + lax.axis_index("tensor")
    ) * units
    peers = lax.axis_size("expert")
    span = EXPERTS * FF // peers
    dest = jnp.arange(peers, dtype=jnp.int32)[:, None]
    intersection = (
        (expert_range[None, :] * FF < (dest + 1) * span)
        & ((expert_range[None, :] + 1) * FF > dest * span)
    ).astype(jnp.float32)
    chosen = jnp.sum(picked, axis=1)
    needed = jnp.dot(intersection, chosen.T, preferred_element_type=jnp.float32) > 0.5
    outgoing = jnp.where(needed[:, :, None], normed[None], jnp.zeros_like(normed)[None])
    out_coefs = jnp.broadcast_to(coefs[None], (peers, coefs.shape[0], coefs.shape[1]))
    rows_in = lax.all_to_all(outgoing, "expert", split_axis=0, concat_axis=0, tiled=True)
    coefs_in = lax.all_to_all(out_coefs, "expert", split_axis=0, concat_axis=0, tiled=True)
    flat_rows = rows_in.reshape(-1, rows_in.shape[2])
    flat_coefs = coefs_in.reshape(-1, coefs_in.shape[2])
    result = expert_terms(flat_rows, flat_coefs, first_unit, gate_weight, up_weight, down_weight)
    partial_value = result.reshape(rows_in.shape[0], rows_in.shape[1], rows_in.shape[2])
    returned = lax.all_to_all(partial_value, "expert", split_axis=0, concat_axis=0, tiled=True)
    routed = lax.psum(jnp.sum(returned, axis=0), "tensor")
    layer_out = (hidden_state.astype(jnp.float32) + routed).astype(jnp.bfloat16)
    return (layer_out, state_next.astype(jnp.bfloat16))


LANES = 128
BLOCK = 384
PLAIN = 128
SLOTS = 2
EPS = 1e-05
VMEM = pl.BlockSpec(memory_space=pltpu.VMEM)
SMEM = pl.BlockSpec(memory_space=pltpu.SMEM)
ANY = pl.BlockSpec(memory_space=pl.ANY)


def beside(bytes_accessed):
    return pl.CostEstimate(flops=bytes_accessed * 300, bytes_accessed=bytes_accessed, transcendentals=0)


F32 = jnp.float32
BF16 = jnp.bfloat16


def lane_to_sublane(row):
    n = row.shape[1]
    spread = jnp.broadcast_to(row, (n, n))
    diagonal = lax.broadcasted_iota(jnp.int32, (n, n), 0) == lax.broadcasted_iota(
        jnp.int32, (n, n), 1
    )
    return jnp.sum(jnp.where(diagonal, spread, 0.0), axis=1, keepdims=True)


def mixer_kernel(*refs):
    sources, (new_state, packet) = refs[:16], refs[16:18]
    buffers, sems = refs[18:34], refs[34]
    copies = [
        pltpu.make_async_copy(source, buffer, sems.at[i])
        for i, (source, buffer) in enumerate(zip(sources, buffers))
    ]
    for copy in copies:
        copy.start()
    late = (7, 12)
    for i, copy in enumerate(copies):
        if i not in late:
            copy.wait()
    (
        slot_ref,
        ids_ref,
        conv_input,
        gate_input,
        step_input,
        b_proj,
        c_proj,
        state_pool,
        conv_pool,
        conv_weight,
        conv_bias,
        step_bias,
        a_log,
        d_skip,
        residual,
        probs,
    ) = buffers
    rows, channels = conv_input.shape
    peers = packet.shape[0]
    cols = residual.shape[1] // peers
    first_slot = lax.axis_index("expert") * state_pool.shape[0]
    lane = lax.broadcasted_iota(jnp.int32, (1, LANES), 1)
    row = lax.broadcasted_iota(jnp.int32, (rows, channels), 0)
    slots = [slot_ref[r] - first_slot for r in range(rows)]
    conv = conv_weight[-1:, :] * conv_input[...].astype(F32) + conv_bias[...]
    for lag in range(conv_pool.shape[0]):
        past = conv_pool[lag].astype(F32)
        history = jnp.zeros((rows, channels), F32)
        for r in range(rows):
            for p in range(past.shape[0]):
                taken = (row == r) & (slots[r] == p)
                history = jnp.where(taken, past[p : p + 1, :], history)
        conv = conv + conv_weight[lag : lag + 1, :] * history
    conv_outs = conv * jax.nn.sigmoid(conv)
    steps = jax.nn.softplus(step_input[...].astype(F32) + step_bias[...])
    drives = steps * conv_outs
    gates = gate_input[...].astype(F32)
    gates = gates * jax.nn.sigmoid(gates)
    skips = d_skip[...] * conv_outs
    for i in late:
        copies[i].wait()
    rates = -jnp.exp(a_log[...])
    for r in range(rows):
        b = lane_to_sublane(b_proj[r : r + 1, :])
        c = lane_to_sublane(c_proj[r : r + 1, :])
        past = state_pool[slots[r]].astype(F32)
        state = jnp.exp(steps[r : r + 1, :] * rates) * past + drives[r : r + 1, :] * b
        new_state[r] = state.astype(BF16)
        output = jnp.sum(c * state, axis=0, keepdims=True) + skips[r : r + 1, :]
        gated = (output * gates[r : r + 1, :]).astype(BF16)
        coefs = jnp.zeros((1, LANES), F32)
        prob = probs[r : r + 1, :].astype(F32)
        for k in range(ids_ref.shape[1]):
            coefs = coefs + jnp.where(lane == ids_ref[r, k], prob[:, k : k + 1], 0.0)
        coefs = coefs.astype(BF16)
        for d in range(peers):
            packet[d, r : r + 1, 0:channels] = gated
            packet[d, r : r + 1, channels : channels + cols] = residual[
                r : r + 1, d * cols : (d + 1) * cols
            ]
            packet[d, r : r + 1, channels + cols :] = coefs


def project_kernel(packets, out_weight, partial, residual_block, coefs, rows_scratch):
    peers, rows, _ = packets.shape
    channels, cols = out_weight.shape
    for d in range(peers):
        rows_scratch[d * rows : (d + 1) * rows, :] = packets[d].astype(F32)
    partial[...] = jnp.dot(
        rows_scratch[:, 0:channels].astype(BF16), out_weight[...], preferred_element_type=F32
    )
    residual_block[...] = rows_scratch[:, channels : channels + cols]
    coefs[...] = rows_scratch[:, channels + cols :]


def hidden_kernel(mine, other, residual_block, copies):
    mixed = (mine[...] + other[...]).astype(BF16).astype(F32)
    hidden = (residual_block[...] + mixed).astype(BF16)
    for d in range(copies.shape[0]):
        copies[d] = hidden


def expert_kernel(
    hidden,
    coefs,
    gain,
    gate_weight,
    up_weight,
    down_hbm,
    partial,
    own_rows,
    turned,
    down_buf,
    wide,
    normed,
    units_out,
    down_sem,
):
    units, width = gate_weight.shape
    peers, rows, cols = hidden.shape
    steps = units // BLOCK
    slots = down_buf.shape[0]

    def down_copy(step):
        slot = lax.rem(step, slots)
        rows = pl.ds(step * BLOCK, BLOCK)
        return pltpu.make_async_copy(down_hbm.at[rows], down_buf.at[slot], down_sem.at[slot])

    def start_copy(i, carry):
        down_copy(i).start()
        return carry

    lax.fori_loop(0, slots, start_copy, 0)
    rest = BLOCK - PLAIN

    def turn(step):
        part = pl.ds(step * BLOCK + PLAIN, rest)
        turned[step % 2, :, 0:rest] = gate_weight[part, :].T
        turned[step % 2, :, rest:] = up_weight[part, :].T

    for d in range(peers):
        wide[:, d * cols : (d + 1) * cols] = hidden[d].astype(F32)
    mean = jnp.sum(wide[...] * wide[...], axis=1, keepdims=True) * (1.0 / width)
    normed[...] = (wide[...] * lax.rsqrt(mean + EPS) * gain[...]).astype(BF16)
    expert = lax.axis_index("expert")
    own = own_rows.shape[0]
    mine = wide[0:own, :]
    for d in range(1, peers):
        mine = jnp.where(expert == d, wide[d * own : (d + 1) * own, :], mine)
    own_rows[...] = mine

    first_unit = (expert * lax.axis_size("tensor") + lax.axis_index("tensor")) * units
    lower = first_unit // FF
    boundary = (lower + 1) * FF - first_unit
    lane = lax.broadcasted_iota(jnp.int32, coefs.shape, 1)
    lower_coef = jnp.sum(jnp.where(lane == lower, coefs[...], 0.0), axis=1, keepdims=True)
    upper_coef = jnp.sum(jnp.where(lane == lower + 1, coefs[...], 0.0), axis=1, keepdims=True)
    dims = (((1,), (1,)), ((), ()))

    def finish(start, gate, up):
        column = lax.broadcasted_iota(jnp.int32, gate.shape, 1) + start
        coef = jnp.where(column < boundary, lower_coef, upper_coef)
        hidden_units = gate * jax.nn.sigmoid(gate) * up * coef
        units_out[:, start : start + gate.shape[1]] = hidden_units.astype(BF16)

    total = wide

    def unit_step(step):
        start = step * BLOCK
        if step + 1 < steps:
            turn(step + 1)
        part = pl.ds(start, BLOCK if step == 0 else PLAIN)
        gate = lax.dot_general(normed[...], gate_weight[part, :], dims, preferred_element_type=F32)
        up = lax.dot_general(normed[...], up_weight[part, :], dims, preferred_element_type=F32)
        finish(start, gate, up)
        if step == 0:
            return
        both = jnp.dot(normed[...], turned[step % 2], preferred_element_type=F32)
        finish(start + PLAIN, both[:, 0:rest], both[:, rest:])

    def down_step(step):
        product = jnp.dot(
            units_out[:, step * BLOCK : (step + 1) * BLOCK],
            down_buf[step % slots],
            preferred_element_type=F32,
        )
        total[...] = product if step == 0 else total[...] + product

    for step in range(steps + 1):
        if step > 0:
            down_copy(step - 1).wait()

        @pl.when(lower >= 0)
        def _():
            if step > 0:
                down_step(step - 1)
            if step < steps:
                unit_step(step)

        if step > 0 and step - 1 + slots < steps:
            down_copy(step - 1 + slots).start()

    for d in range(peers):
        partial[d] = total[d * own : (d + 1) * own, :].astype(BF16)


def sum_kernel(pieces, out):
    total = pieces[0].astype(F32)
    for d in range(1, pieces.shape[0]):
        total = total + pieces[d].astype(F32)
    out[...] = total


def output_kernel(mine, other, own_rows, out):
    out[...] = (own_rows[...] + (mine[...] + other[...])).astype(BF16)


def run_experts(hidden, coefs, norm_gain, gate_weight, up_weight, down_weight):
    peers, all_rows, cols = hidden.shape
    units, width = gate_weight.shape
    rows = all_rows // peers
    shape = jax.ShapeDtypeStruct
    return pl.pallas_call(
        expert_kernel,
        out_shape=(
            shape((peers, rows, width), BF16),
            shape((rows, width), F32),
        ),
        in_specs=[VMEM] * 5 + [ANY],
        out_specs=(VMEM, VMEM),
        scratch_shapes=[
            pltpu.VMEM((2, width, 2 * (BLOCK - PLAIN)), BF16),
            pltpu.VMEM((SLOTS, BLOCK, width), BF16),
            pltpu.VMEM((all_rows, width), F32),
            pltpu.VMEM((all_rows, width), BF16),
            pltpu.VMEM((all_rows, units), BF16),
            pltpu.SemaphoreType.DMA((SLOTS,)),
        ],
        compiler_params=pltpu.CompilerParams(vmem_limit_bytes=17 * 2**20),
        name="experts",
    )(
        hidden,
        coefs,
        norm_gain[None],
        pltpu.with_memory_space_constraint(gate_weight, pltpu.VMEM),
        pltpu.with_memory_space_constraint(up_weight, pltpu.VMEM),
        down_weight,
    )


def run_mixer(peers, cols, conv_input, gate_input, step_input, b_proj, c_proj, slot_ids, state_pool, conv_pool, conv_weight, conv_bias, step_bias, a_log, d_skip, residual, expert_ids, expert_probs):
    rows, channels = conv_input.shape
    packet_width = channels + cols + LANES
    shape = jax.ShapeDtypeStruct
    mixer_inputs = (
        slot_ids,
        expert_ids,
        conv_input,
        gate_input,
        step_input,
        b_proj,
        c_proj,
        state_pool,
        jnp.transpose(conv_pool, (1, 0, 2)),
        conv_weight,
        conv_bias[None],
        step_bias[None],
        a_log,
        d_skip[None],
        residual,
        expert_probs,
    )
    return pl.pallas_call(
        mixer_kernel,
        out_shape=(
            pltpu.VMEM((rows,) + state_pool.shape[1:], BF16),
            shape((peers, rows, packet_width), BF16),
        ),
        in_specs=[ANY] * len(mixer_inputs),
        out_specs=(VMEM, VMEM),
        scratch_shapes=[pltpu.SMEM(x.shape, x.dtype) for x in mixer_inputs[:2]]
        + [pltpu.VMEM(x.shape, x.dtype) for x in mixer_inputs[2:]]
        + [pltpu.SemaphoreType.DMA((len(mixer_inputs),))],
        compiler_params=pltpu.CompilerParams(vmem_limit_bytes=6 * 2**20),
        cost_estimate=beside(300000000),
        name="mixer",
    )(*(pltpu.with_memory_space_constraint(x, pltpu.HBM) for x in mixer_inputs))


def fused(
    conv_input,
    gate_input,
    step_input,
    b_proj,
    c_proj,
    slot_ids,
    state_pool,
    conv_pool,
    conv_weight,
    conv_bias,
    step_bias,
    a_log,
    d_skip,
    out_weight,
    residual,
    norm_gain,
    expert_ids,
    expert_probs,
    gate_weight,
    up_weight,
    down_weight,
):
    rows, channels = conv_input.shape
    width = residual.shape[1]
    units = gate_weight.shape[0]
    cols = out_weight.shape[1]
    peers = lax.axis_size("expert")
    halves = lax.axis_size("tensor")
    all_rows = peers * rows
    shape = jax.ShapeDtypeStruct
    packet_width = channels + cols + LANES

    new_state, packet = run_mixer(
        peers,
        cols,
        conv_input,
        gate_input,
        step_input,
        b_proj,
        c_proj,
        slot_ids,
        state_pool,
        conv_pool,
        conv_weight,
        conv_bias,
        step_bias,
        a_log,
        d_skip,
        residual,
        expert_ids,
        expert_probs,
    )
    packets = lax.all_to_all(packet, "expert", split_axis=0, concat_axis=0, tiled=True)
    partial_mixed, residual_block, coefs = pl.pallas_call(
        project_kernel,
        out_shape=(
            shape((all_rows, cols), F32),
            shape((all_rows, cols), F32),
            shape((all_rows, LANES), F32),
        ),
        in_specs=[VMEM] * 2,
        out_specs=(VMEM,) * 3,
        scratch_shapes=[pltpu.VMEM((all_rows, packet_width), F32)],
        compiler_params=pltpu.CompilerParams(vmem_limit_bytes=6 * 2**20),
        cost_estimate=beside(300000000),
        name="project",
    )(packets, out_weight)
    swap = [(i, halves - 1 - i) for i in range(halves)]
    other_mixed = lax.ppermute(partial_mixed, "tensor", swap)
    hidden_copies = pl.pallas_call(
        hidden_kernel,
        out_shape=shape((peers, all_rows, cols), BF16),
        in_specs=[VMEM] * 3,
        out_specs=VMEM,
        compiler_params=pltpu.CompilerParams(vmem_limit_bytes=2 * 2**20),
        cost_estimate=beside(150000000),
        name="hidden",
    )(partial_mixed, other_mixed, residual_block)
    hidden = lax.all_to_all(hidden_copies, "expert", split_axis=0, concat_axis=0, tiled=True)
    partial_out, own_rows = run_experts(
        hidden, coefs, norm_gain, gate_weight, up_weight, down_weight
    )
    pieces = lax.all_to_all(partial_out, "expert", split_axis=0, concat_axis=0, tiled=True)
    routed = pl.pallas_call(
        sum_kernel,
        out_shape=shape((rows, width), F32),
        in_specs=[VMEM],
        out_specs=VMEM,
        compiler_params=pltpu.CompilerParams(vmem_limit_bytes=2 * 2**20),
        name="sum",
    )(pieces)
    other_routed = lax.ppermute(routed, "tensor", swap)
    layer_out = pl.pallas_call(
        output_kernel,
        out_shape=shape((rows, width), BF16),
        in_specs=[VMEM] * 3,
        out_specs=VMEM,
        compiler_params=pltpu.CompilerParams(vmem_limit_bytes=2 * 2**20),
        name="output",
    )(routed, other_routed, own_rows)
    return (layer_out, new_state)


def body(*args):
    out_weight, gate_weight = args[13], args[18]
    tiled = (
        out_weight.shape[1] % LANES == 0
        and gate_weight.shape[0] % BLOCK == 0
        and gate_weight.shape[0] // BLOCK >= SLOTS
        and lax.axis_size("tensor") == 2
    )
    return fused(*args) if tiled else local(*args)


def solution(mesh):
    return jax.shard_map(
        body,
        mesh=mesh,
        in_specs=(
            P(("groups", "expert"), "tensor"),
            P(("groups", "expert"), "tensor"),
            P(("groups", "expert"), "tensor"),
            P(("groups", "expert"), None),
            P(("groups", "expert"), None),
            P(("groups", "expert")),
            P(("groups", "expert"), None, "tensor"),
            P(("groups", "expert"), None, "tensor"),
            P(None, "tensor"),
            P("tensor"),
            P("tensor"),
            P(None, "tensor"),
            P("tensor"),
            P("tensor", "expert"),
            P(("groups", "expert"), None),
            P(),
            P(("groups", "expert"), None),
            P(("groups", "expert"), None),
            P(("expert", "tensor"), None),
            P(("expert", "tensor"), None),
            P(("expert", "tensor"), None),
        ),
        out_specs=(P(("groups", "expert"), None), P(("groups", "expert"), None, "tensor")),
        check_vma=False,
    )
```
